32 devices in a mesh: groups: 2 (over y), dp: 4 (over z), mp: 4 (over x, core).
Axes of the slice: x: 2, y: 2, z: 4, core: 2. Of those that a mesh axis runs over, the one named last changes fastest.
Arguments:
- activations: bfloat16 [16, 128, 28672], P(('groups', 'dp'), None, 'mp'), parts along dimension 0
- output_gradients: bfloat16 [16, 128, 8192], P(('groups', 'dp'), None, 'mp'), parts along dimension 0
- counts: int32 [16], P(('groups', 'dp')), parts along dimension 0, may hold values from 32 to 128, as said below
- left_factors: bfloat16 [256, 8192], P('dp', 'mp'), may hold values from -0.0625 to 0.0625
- right_factors: bfloat16 [256, 28672], P('dp', 'mp'), may hold values from -0.03125 to 0.03125
Outputs:
- scores: float32 [16, 8], P(('groups', 'dp')), parts along dimension 0
- grad_rms: float32 [16], P(('groups', 'dp')), parts along dimension 0
The draws below stay inside these ranges and needn't reach their ends.
There are 2 independent parts, one for each index of `groups`. The reference program is written for one: setup_inputs(seed, part) draws one part's arguments, and reference() takes and returns one part's arrays. A program takes and returns all parts, laid end to end along the dimension named above; an argument that names none is the same for every part. Nothing has to cross between parts.
Inputs may be any that keep to these rules, and one draw needn't show every extreme that they name: `counts`: some training sequence has all 128 slots filled and some has 32.
All inputs are finite; a program needn't handle non-finite values.
Results may differ from the reference program's by a relative error of at most 0.0003.
Values may be sent and summed in bfloat16 or wider, within the bound.
A program may use at most 64 MiB of HBM per device.

```python
import math
import jax
import jax.numpy as jnp
from jax import lax

D = 8192
FF = 28672
RANK = 32
QUERIES = 8
LEN = 128
SEQS = 8
QCOLS = 256


def feature_scales(key, row_count, width, spread):
    key_rows, key_cols = jax.random.split(key)
    row_scale = jnp.exp(jax.random.uniform(key_rows, (row_count, 1), jnp.float32, 0.0, math.log(spread)))
    rising = math.log(3.0) * jnp.arange(width, dtype=jnp.float32) / width
    col_scale = jnp.exp(jax.random.uniform(key_cols, (1, width), jnp.float32, 0.0, math.log(spread)) + rising[None, :])
    return row_scale * col_scale


def feature_draw(key, width, spread):
    key_base = jax.random.fold_in(key, 0)
    key_scale = jax.random.fold_in(key, 2)
    row_count = SEQS * LEN
    base = jax.random.normal(key_base, (row_count, width), jnp.float32)
    scaled = 0.25 * base * feature_scales(key_scale, row_count, width, spread)
    return scaled.reshape(SEQS, LEN, width)


def draw_activations(key, part):
    key = jax.random.fold_in(key, 11)
    values = feature_draw(key, FF, 10.0)
    return values.astype(jnp.bfloat16)


def draw_output_gradients(key, part):
    key = jax.random.fold_in(key, 23)
    values = feature_draw(key, D, 10.0)
    return values.astype(jnp.bfloat16)


def draw_counts(key, part):
    key = jax.random.fold_in(key, 5)
    filled = jax.random.randint(key, (SEQS,), LEN // 4, LEN + 1)
    filled = filled.at[0].set(LEN)
    filled = filled.at[1].set(LEN // 4)
    return filled.astype(jnp.int32)


def steps_of(key, dims, shards, low, top_value):
    level, own = 1.0, jax.random.fold_in(key, 6)
    for dim, parts in shards:
        heights = jnp.exp(jax.random.uniform(jax.random.fold_in(own, dim), (parts,), jnp.float32, low / len(shards), top_value / len(shards)))
        level = level * jnp.repeat(heights, dims[dim] // parts).reshape([-1 if axis == dim else 1 for axis in range(len(dims))])
    return level


def noise(rng, dims, scale, reach, shards=(), held_as=jnp.bfloat16):
    result = scale * jax.random.normal(rng, dims, jnp.float32)
    if shards:
        result = result * steps_of(rng, dims, shards, -0.22, 0.18)
    return jnp.clip(result, -reach, reach).astype(held_as)


def setup_inputs(seed: int = 0, part: int = 0) -> dict:
    seeds = jax.random.split(jax.random.key(seed), 6)
    part_keys = jax.random.split(jax.random.fold_in(seeds[5], part), 6)
    return {
        "activations": draw_activations(jax.random.fold_in(jax.random.fold_in(seeds[5], part), 71), part),
        "output_gradients": draw_output_gradients(jax.random.fold_in(jax.random.fold_in(seeds[5], part), 71), part),
        "counts": draw_counts(jax.random.fold_in(jax.random.fold_in(seeds[5], part), 71), part),
        "left_factors": noise(seeds[3], (QCOLS, D), D ** -0.5, 0.0625, ((0, 4), (1, 4))),
        "right_factors": noise(seeds[4], (QCOLS, FF), FF ** -0.5, 0.03125, ((0, 4), (1, 4))),
    }


epsilon = 1e-06

def reference(activations, output_gradients, counts, left_factors, right_factors):

    def one_sequence(items):
        activity, gradient, token_count = items
        slots = jnp.arange(LEN, dtype=jnp.int32)
        token_mask = (slots < token_count).astype(jnp.float32)
        grad_proj = jnp.dot(gradient, left_factors.T, preferred_element_type=jnp.float32)
        act_proj = jnp.dot(activity, right_factors.T, preferred_element_type=jnp.float32)
        token_terms = grad_proj * act_proj * token_mask[:, None]
        raw_score = lax.optimization_barrier(jnp.sum(token_terms, axis=0)).reshape(QUERIES, RANK).sum(axis=1)
        gradient_covariance = jnp.dot(gradient, gradient.T, preferred_element_type=jnp.float32)
        act_gram = jnp.dot(activity, activity.T, preferred_element_type=jnp.float32)
        pair_mask = token_mask[:, None] * token_mask[None, :]
        norm_sq = jnp.sum(gradient_covariance * act_gram * pair_mask)
        return (raw_score, norm_sq)
    raw_score, norm_sq = lax.map(one_sequence, (activations, output_gradients, counts))
    grad_rms = jnp.sqrt(norm_sq / (D * FF) + epsilon)
    return (raw_score / grad_rms[:, None], grad_rms)
```

```python
import functools

import jax
import jax.numpy as jnp
from jax import lax
from jax.experimental import pallas as pl
from jax.experimental.pallas import tpu as pltpu
from jax.sharding import PartitionSpec as P

D = 8192
FF = 28672
RANK = 32
AHEAD = 3
SWAP = 2

epsilon = 1e-06
MESH = pl.DeviceIdType.MESH


def contract_last(left_side, right_side):
    return lax.dot_general(
        left_side, right_side, (((1,), (1,)), ((), ())), preferred_element_type=jnp.float32
    )


def plain_shards(activations, output_gradients, counts, left_factors, right_factors):
    seq_dev, length, ff_local = activations.shape
    local_model_width = output_gradients.shape[2]
    row_count = seq_dev * length
    act_rows = activations.reshape(row_count, ff_local)
    grad_rows = output_gradients.reshape(row_count, local_model_width)
    qcols_all = left_factors.shape[0] * lax.axis_size("dp")
    positions = lax.broadcasted_iota(jnp.int32, (seq_dev, length), 1)
    token_mask = (positions < counts[:, None]).astype(jnp.float32)
    pair_mask = token_mask[:, :, None] * token_mask[:, None, :]
    token_mask = token_mask.reshape(row_count)
    left_all, right_all = (
        lax.all_gather(left_factors, "dp", axis=0, tiled=True),
        lax.all_gather(right_factors, "dp", axis=0, tiled=True),
    )
    grad_proj = contract_last(grad_rows, left_all)
    act_proj = contract_last(act_rows, right_all)
    gradient_covariance = jnp.einsum(
        "anr,ayr->any", output_gradients, output_gradients, preferred_element_type=jnp.float32
    )
    act_gram = jnp.einsum(
        "slf,smf->slm", activations, activations, preferred_element_type=jnp.float32
    )
    grad_proj, gradient_covariance = lax.psum((grad_proj, gradient_covariance), "mp")
    token_terms = grad_proj * act_proj * token_mask[:, None]
    score_part = token_terms.reshape(seq_dev, length, qcols_all // RANK, RANK).sum(axis=(1, 3))
    norm_portion = jnp.sum(gradient_covariance * act_gram * pair_mask, axis=(1, 2))
    raw_score, norm_sq = lax.psum((score_part, norm_portion), "mp")
    grad_rms = jnp.sqrt(norm_sq / (D * FF) + epsilon)
    return (raw_score / grad_rms[:, None], grad_rms)


def line_kernel(
    n_left, n_right, width,
    counts_ref, act_ref, grad_ref, left_ref, right_ref,
    scores_ref, rms_ref,
    factors, rows, proj, gram, proj_in, gram_in, tile, tile_in,
    own_sem, row_sem, out_send, in_send, line_recv, swap_send, swap_recv,
    proj_send, proj_recv, gram_send, gram_recv, tile_send, tile_recv,
):
    pieces = n_left + n_right
    g, z, m = lax.axis_index("groups"), lax.axis_index("dp"), lax.axis_index("mp")
    other = 1 - g
    step_in = 1 - 2 * (z // 2)
    inner = ((z + 1) // 2) % 2
    is_inner = inner == 1
    inward, outward = z + step_in, z - step_in
    peers = [lax.rem(m + i, 4) for i in (1, 2, 3)]

    def offset(half, piece):
        if piece < n_left:
            return (half * n_left + piece) * width
        return (half * n_right + piece - n_left) * width

    def factor_copy(half, piece):
        source, at = left_ref if piece < n_left else right_ref, offset(half, piece)
        return pltpu.make_async_copy(
            source.at[:, at:at + width], factors.at[z, half, piece], own_sem.at[half, piece]
        )

    def row_copy(half, piece):
        source, at = grad_ref if piece < n_left else act_ref, offset(half, piece)
        return pltpu.make_async_copy(
            source.at[:, at:at + width], rows.at[half, piece], row_sem.at[half, piece]
        )

    everything = [(half, piece) for piece in range(pieces) for half in range(2)]
    for half, piece in everything:
        factor_copy(half, piece).start()
    for half, piece in everything:
        row_copy(half, piece).start()

    barrier = pltpu.get_barrier_semaphore()
    for i in range(3):
        pl.semaphore_signal(barrier, inc=1, device_id=(g, z, peers[i]), device_id_type=MESH)
    pl.semaphore_signal(barrier, inc=1, device_id=(other, z, m), device_id_type=MESH)
    pl.semaphore_signal(barrier, inc=1, device_id=(g, inward, m), device_id_type=MESH)

    @pl.when(is_inner)
    def _():
        pl.semaphore_signal(barrier, inc=1, device_id=(g, outward, m), device_id_type=MESH)

    proj[...] = jnp.zeros_like(proj)
    gram[...] = jnp.zeros_like(gram)
    pl.semaphore_wait(barrier, 5 + inner)
    for half, piece in everything:
        factor_copy(half, piece).wait()

    def outward_copy(k):
        block = factors.at[(z + (k // pieces) * step_in) % 4, g, k % pieces]
        return pltpu.make_async_remote_copy(
            src_ref=block, dst_ref=block, send_sem=out_send.at[k], recv_sem=line_recv.at[0, k],
            device_id=(g, (outward + 4) % 4, m), device_id_type=MESH,
        )

    def inward_copy(k):
        late = k // pieces
        source = (z - late * inner * step_in + 4) % 4
        half = g + (1 - inner) * late * (1 - 2 * g)
        block = factors.at[source, half, k % pieces]
        return pltpu.make_async_remote_copy(
            src_ref=block, dst_ref=block, send_sem=in_send.at[k],
            recv_sem=line_recv.at[1 - inner, k],
            device_id=(g, inward, m), device_id_type=MESH,
        )

    def main_source(k):
        return (z + (k // pieces + 1) * step_in + 4) % 4

    def arrival(k):
        block = factors.at[main_source(k), g, k % pieces]
        return pltpu.make_async_remote_copy(
            src_ref=block, dst_ref=block, send_sem=out_send.at[k], recv_sem=line_recv.at[0, k],
            device_id=(g, inward, m), device_id_type=MESH,
        )

    def minor_arrival(k):
        late = k // pieces
        block = factors.at[(outward + 4) % 4, g + late * (1 - 2 * g), k % pieces]
        return pltpu.make_async_remote_copy(
            src_ref=block, dst_ref=block, send_sem=out_send.at[k], recv_sem=line_recv.at[1, k],
            device_id=(g, inward, m), device_id_type=MESH,
        )

    def swap_copy(k):
        block = factors.at[main_source(k), g, k % pieces]
        return pltpu.make_async_remote_copy(
            src_ref=block, dst_ref=block, send_sem=swap_send.at[k], recv_sem=swap_recv.at[k],
            device_id=(other, z, m), device_id_type=MESH,
        )

    def swap_arrival(k):
        block = factors.at[main_source(k), other, k % pieces]
        return pltpu.make_async_remote_copy(
            src_ref=block, dst_ref=block, send_sem=swap_send.at[k], recv_sem=swap_recv.at[k],
            device_id=(other, z, m), device_id_type=MESH,
        )

    def proj_copy(i, source):
        return pltpu.make_async_remote_copy(
            src_ref=proj.at[0, source], dst_ref=proj_in.at[i, source],
            send_sem=proj_send.at[i, source], recv_sem=proj_recv.at[i, source],
            device_id=(g, z, peers[i]), device_id_type=MESH,
        )

    def gram_copy(i):
        return pltpu.make_async_remote_copy(
            src_ref=gram.at[0], dst_ref=gram_in.at[i],
            send_sem=gram_send.at[i], recv_sem=gram_recv.at[i],
            device_id=(g, z, peers[i]), device_id_type=MESH,
        )

    def tile_copy(i):
        return pltpu.make_async_remote_copy(
            src_ref=tile, dst_ref=tile_in.at[i],
            send_sem=tile_send.at[i], recv_sem=tile_recv.at[i],
            device_id=(g, z, peers[i]), device_id_type=MESH,
        )

    def project(source, piece):
        part = contract_last(factors[source, 0, piece], rows[0, piece])
        part += contract_last(factors[source, 1, piece], rows[1, piece])
        side = (piece + pieces - n_left) // pieces
        proj[side, source] += part

    length = rows.shape[2] // 2
    total = 3 * pieces

    def step(k, carry):
        @pl.when(k < total)
        def _():
            @pl.when(is_inner)
            def _():
                @pl.when(k >= AHEAD)
                def _():
                    outward_copy(k - AHEAD).wait_send()
                outward_copy(k).start()

            @pl.when((k >= AHEAD) & (k < 2 * pieces + AHEAD))
            def _():
                inward_copy(k - AHEAD).wait_send()

            @pl.when(k < 2 * pieces)
            def _():
                inward_copy(k).start()

        @pl.when((k >= AHEAD) & (k < total + AHEAD))
        def _():
            j = k - AHEAD

            @pl.when(j < 2 * pieces + (1 - inner) * pieces)
            def _():
                arrival(j).wait_recv()
                swap_copy(j).start()

            @pl.when(j < 2 * pieces * inner)
            def _():
                minor_arrival(j).wait_recv()

        @pl.when(k < pieces)
        def _():
            for half in range(2):
                pltpu.make_async_copy(
                    grad_ref.at[:, 0:width], rows.at[half, k], row_sem.at[half, k]
                ).wait()
            project(z, k)
            side = (k + pieces - n_left) // pieces
            for seq in range(2):
                span = slice(seq * length, (seq + 1) * length)
                first, second = rows[0, k, span, :], rows[1, k, span, :]
                gram[side, span, :] += contract_last(first, first) + contract_last(second, second)

        @pl.when(k == n_left - 1)
        def _():
            for i in range(3):
                proj_copy(i, z).start()
                gram_copy(i).start()

        @pl.when(k >= AHEAD + SWAP)
        def _():
            j = k - AHEAD - SWAP

            @pl.when(j < 2 * pieces + (1 - inner) * pieces)
            def _():
                swap_copy(j).wait_send()
                swap_arrival(j).wait_recv()
            project(main_source(j), j % pieces)

            @pl.when(j % pieces == n_left - 1)
            def _():
                for i in range(3):
                    proj_copy(i, main_source(j)).start()
        return carry

    lax.fori_loop(0, total + AHEAD + SWAP, step, 0)

    token = lax.broadcasted_iota(jnp.int32, (1, length), 1)
    masks = [(token < counts_ref[seq]).astype(jnp.float32) for seq in range(2)]
    row_token = lax.broadcasted_iota(jnp.int32, (length, 1), 0)
    row_masks = [(row_token < counts_ref[seq]).astype(jnp.float32) for seq in range(2)]
    for i in range(3):
        gram_copy(i).wait_recv()
    norms = []
    for seq in range(2):
        span = slice(seq * length, (seq + 1) * length)
        whole = gram[0, span, :] + gram_in[0, span, :] + gram_in[1, span, :] + gram_in[2, span, :]
        terms = whole * gram[1, span, :] * masks[seq]
        down = jnp.sum(terms * row_masks[seq], axis=0, keepdims=True)
        norms.append(jnp.sum(down, axis=1, keepdims=True))
    for i in range(3):
        for source in range(4):
            proj_copy(i, source).wait_recv()
    columns = proj.shape[2]
    queries = 4 * columns // RANK
    mask_row = jnp.concatenate(masks, axis=1)
    lane = lax.broadcasted_iota(jnp.int32, (1, 128), 1)
    found = [jnp.zeros((1, 128), jnp.float32) for _ in range(2)]
    for source in range(4):
        whole = proj[0, source] + proj_in[0, source] + proj_in[1, source] + proj_in[2, source]
        terms = whole * proj[1, source] * mask_row
        for q in range(columns // RANK):
            down = jnp.sum(terms[q * RANK:(q + 1) * RANK, :], axis=0, keepdims=True)
            for seq in range(2):
                value = jnp.sum(down[:, seq * length:(seq + 1) * length], axis=1, keepdims=True)
                found[seq] += jnp.where(lane == source * (columns // RANK) + q, value, 0.0)
    tile[...] = jnp.concatenate(
        found + [jnp.broadcast_to(norms[seq], (1, 128)) for seq in range(2)]
        + [jnp.zeros((4, 128), jnp.float32)], axis=0
    )
    for i in range(3):
        tile_copy(i).start()
    for i in range(3):
        tile_copy(i).wait_recv()
    whole = tile[...] + tile_in[0] + tile_in[1] + tile_in[2]
    rms = jnp.sqrt(whole[2:4, :] / (D * FF) + epsilon)
    scores_ref[...] = (whole[0:2, :] / rms)[:, 0:queries]
    rms_ref[...] = jnp.where(lane == 0, rms[0:1, :], rms[1:2, :])[:, 0:2]

    for k in range(AHEAD):
        @pl.when(is_inner)
        def _():
            outward_copy(total - 1 - k).wait_send()
    for i in range(3):
        tile_copy(i).wait_send()
        gram_copy(i).wait_send()
        for source in range(4):
            proj_copy(i, source).wait_send()


def piece_width(model_width, hidden_width):
    for width in (512, 256, 128):
        if model_width % (2 * width) == 0 and hidden_width % (2 * width) == 0:
            return width
    return 0


def line_shards(width, activations, output_gradients, counts, left_factors, right_factors):
    seq_dev, length, ff_local = activations.shape
    model_local = output_gradients.shape[2]
    row_count = seq_dev * length
    columns = left_factors.shape[0]
    n_left, n_right = model_local // (2 * width), ff_local // (2 * width)
    pieces = n_left + n_right
    dma = pltpu.SemaphoreType.DMA
    anywhere = pl.BlockSpec(memory_space=pl.ANY)
    vmem = pl.BlockSpec(memory_space=pltpu.VMEM)
    scores, rms = pl.pallas_call(
        functools.partial(line_kernel, n_left, n_right, width),
        out_shape=(
            jax.ShapeDtypeStruct((seq_dev, 4 * columns // RANK), jnp.float32),
            jax.ShapeDtypeStruct((1, seq_dev), jnp.float32),
        ),
        in_specs=[pl.BlockSpec(memory_space=pltpu.SMEM)] + [anywhere] * 4,
        out_specs=(vmem, vmem),
        scratch_shapes=[
            pltpu.VMEM((4, 2, pieces, columns, width), jnp.bfloat16),
            pltpu.VMEM((2, pieces, row_count, width), jnp.bfloat16),
            pltpu.VMEM((2, 4, columns, row_count), jnp.float32),
            pltpu.VMEM((2, row_count, length), jnp.float32),
            pltpu.VMEM((3, 4, columns, row_count), jnp.float32),
            pltpu.VMEM((3, row_count, length), jnp.float32),
            pltpu.VMEM((8, 128), jnp.float32),
            pltpu.VMEM((3, 8, 128), jnp.float32),
            dma((2, pieces)),
            dma((2, pieces)),
            dma((3 * pieces,)),
            dma((2 * pieces,)),
            dma((2, 3 * pieces)),
            dma((3 * pieces,)),
            dma((3 * pieces,)),
            dma((3, 4)),
            dma((3, 4)),
            dma((3,)),
            dma((3,)),
            dma((3,)),
            dma((3,)),
        ],
        compiler_params=pltpu.CompilerParams(
            collective_id=0, has_side_effects=True, vmem_limit_bytes=32 * 2 ** 20
        ),
        cost_estimate=pl.CostEstimate(
            flops=2 * row_count * (4 * columns + length) * (model_local + ff_local),
            bytes_accessed=2 * (row_count + columns) * (model_local + ff_local),
            transcendentals=0,
        ),
    )(
        counts,
        activations.reshape(row_count, ff_local),
        output_gradients.reshape(row_count, model_local),
        left_factors,
        right_factors,
    )
    return scores, rms.reshape(seq_dev)


def shards(sizes, activations, output_gradients, counts, left_factors, right_factors):
    columns, model_local = left_factors.shape
    width = piece_width(model_local, right_factors.shape[1])
    fits = (
        sizes == (2, 4, 4)
        and width > 0
        and columns % RANK == 0
        and activations.shape[:2] == (2, 128)
    )
    run = functools.partial(line_shards, width) if fits else plain_shards
    return run(activations, output_gradients, counts, left_factors, right_factors)


def solution(mesh):
    placed = (
        P(("groups", "dp"), None, "mp"),
        P(("groups", "dp"), None, "mp"),
        P(("groups", "dp")),
        P("dp", "mp"),
        P("dp", "mp"),
    )
    sizes = tuple(mesh.shape[name] for name in ("groups", "dp", "mp"))
    return jax.shard_map(
        functools.partial(shards, sizes),
        mesh=mesh,
        in_specs=placed,
        out_specs=(P(("groups", "dp"), None), P(("groups", "dp"))),
        check_vma=False,
    )
```

```python
import functools

import jax
import jax.numpy as jnp
from jax import lax
from jax.experimental import pallas as pl
from jax.experimental.pallas import tpu as pltpu
from jax.sharding import PartitionSpec as P

D = 8192
FF = 28672
RANK = 32
AHEAD = 5
SWAP = 3

epsilon = 1e-06
MESH = pl.DeviceIdType.MESH


def contract_last(left_side, right_side):
    return lax.dot_general(
        left_side, right_side, (((1,), (1,)), ((), ())), preferred_element_type=jnp.float32
    )


def plain_shards(activations, output_gradients, counts, left_factors, right_factors):
    seq_dev, length, ff_local = activations.shape
    local_model_width = output_gradients.shape[2]
    row_count = seq_dev * length
    act_rows = activations.reshape(row_count, ff_local)
    grad_rows = output_gradients.reshape(row_count, local_model_width)
    qcols_all = left_factors.shape[0] * lax.axis_size("dp")
    positions = lax.broadcasted_iota(jnp.int32, (seq_dev, length), 1)
    token_mask = (positions < counts[:, None]).astype(jnp.float32)
    pair_mask = token_mask[:, :, None] * token_mask[:, None, :]
    token_mask = token_mask.reshape(row_count)
    left_all, right_all = (
        lax.all_gather(left_factors, "dp", axis=0, tiled=True),
        lax.all_gather(right_factors, "dp", axis=0, tiled=True),
    )
    grad_proj = contract_last(grad_rows, left_all)
    act_proj = contract_last(act_rows, right_all)
    gradient_covariance = jnp.einsum(
        "anr,ayr->any", output_gradients, output_gradients, preferred_element_type=jnp.float32
    )
    act_gram = jnp.einsum(
        "slf,smf->slm", activations, activations, preferred_element_type=jnp.float32
    )
    grad_proj, gradient_covariance = lax.psum((grad_proj, gradient_covariance), "mp")
    token_terms = grad_proj * act_proj * token_mask[:, None]
    score_part = token_terms.reshape(seq_dev, length, qcols_all // RANK, RANK).sum(axis=(1, 3))
    norm_portion = jnp.sum(gradient_covariance * act_gram * pair_mask, axis=(1, 2))
    raw_score, norm_sq = lax.psum((score_part, norm_portion), "mp")
    grad_rms = jnp.sqrt(norm_sq / (D * FF) + epsilon)
    return (raw_score / grad_rms[:, None], grad_rms)


def line_kernel(
    n_left, n_right, width,
    counts_ref, act_ref, grad_ref, left_ref, right_ref,
    out_ref,
    factors, rows, proj, gram, proj_in, gram_in, full, found, tile, tile_in,
    own_sem, row_sem, out_send, in_send, line_recv, swap_send, swap_recv,
    proj_send, proj_recv, gram_send, gram_recv, tile_send, tile_recv,
):
    pieces = n_left + n_right
    g, z, m = lax.axis_index("groups"), lax.axis_index("dp"), lax.axis_index("mp")
    other = 1 - g
    step_in = 1 - 2 * (z // 2)
    inner = ((z + 1) // 2) % 2
    is_inner = inner == 1
    inward, outward = z + step_in, z - step_in
    peers = [lax.rem(m + i, 4) for i in (1, 2, 3)]

    def offset(half, piece):
        if piece < n_left:
            return (half * n_left + piece) * width
        return (half * n_right + piece - n_left) * width

    def factor_copy(half, piece):
        source, at = left_ref if piece < n_left else right_ref, offset(half, piece)
        return pltpu.make_async_copy(
            source.at[:, at:at + width], factors.at[z, half, piece], own_sem.at[half, piece]
        )

    def row_copy(half, piece):
        source, at = grad_ref if piece < n_left else act_ref, offset(half, piece)
        return pltpu.make_async_copy(
            source.at[:, at:at + width], rows.at[half, piece], row_sem.at[half, piece]
        )

    barrier = pltpu.get_barrier_semaphore()
    for i in range(3):
        pl.semaphore_signal(barrier, inc=1, device_id=(g, z, peers[i]), device_id_type=MESH)
    pl.semaphore_signal(barrier, inc=1, device_id=(other, z, m), device_id_type=MESH)
    pl.semaphore_signal(barrier, inc=1, device_id=(g, inward, m), device_id_type=MESH)

    @pl.when(is_inner)
    def _():
        pl.semaphore_signal(barrier, inc=1, device_id=(g, outward, m), device_id_type=MESH)

    everything = [(half, piece) for piece in range(pieces) for half in range(2)]
    for half, piece in everything:
        factor_copy(half, piece).start()
    for half, piece in everything:
        row_copy(half, piece).start()

    proj[...] = jnp.zeros_like(proj)
    gram[...] = jnp.zeros_like(gram)
    pl.semaphore_wait(barrier, 5 + inner)

    def outward_copy(k):
        block = factors.at[(z + (k // pieces) * step_in) % 4, g, k % pieces]
        return pltpu.make_async_remote_copy(
            src_ref=block, dst_ref=block, send_sem=out_send.at[k], recv_sem=line_recv.at[0, k],
            device_id=(g, (outward + 4) % 4, m), device_id_type=MESH,
        )

    def inward_copy(k):
        late = k // pieces
        source = (z - late * inner * step_in + 4) % 4
        half = g + (1 - inner) * late * (1 - 2 * g)
        block = factors.at[source, half, k % pieces]
        return pltpu.make_async_remote_copy(
            src_ref=block, dst_ref=block, send_sem=in_send.at[k],
            recv_sem=line_recv.at[1 - inner, k],
            device_id=(g, inward, m), device_id_type=MESH,
        )

    def main_source(k):
        return (z + (k // pieces + 1) * step_in + 4) % 4

    def arrival(k):
        block = factors.at[main_source(k), g, k % pieces]
        return pltpu.make_async_remote_copy(
            src_ref=block, dst_ref=block, send_sem=out_send.at[k], recv_sem=line_recv.at[0, k],
            device_id=(g, inward, m), device_id_type=MESH,
        )

    def minor_arrival(k):
        late = k // pieces
        block = factors.at[(outward + 4) % 4, g + late * (1 - 2 * g), k % pieces]
        return pltpu.make_async_remote_copy(
            src_ref=block, dst_ref=block, send_sem=out_send.at[k], recv_sem=line_recv.at[1, k],
            device_id=(g, inward, m), device_id_type=MESH,
        )

    def swap_copy(k):
        block = factors.at[main_source(k), g, k % pieces]
        return pltpu.make_async_remote_copy(
            src_ref=block, dst_ref=block, send_sem=swap_send.at[k], recv_sem=swap_recv.at[k],
            device_id=(other, z, m), device_id_type=MESH,
        )

    def swap_arrival(k):
        block = factors.at[main_source(k), other, k % pieces]
        return pltpu.make_async_remote_copy(
            src_ref=block, dst_ref=block, send_sem=swap_send.at[k], recv_sem=swap_recv.at[k],
            device_id=(other, z, m), device_id_type=MESH,
        )

    def proj_copy(i, source):
        return pltpu.make_async_remote_copy(
            src_ref=proj.at[0, source], dst_ref=proj_in.at[i, source],
            send_sem=proj_send.at[i, source], recv_sem=proj_recv.at[i, source],
            device_id=(g, z, peers[i]), device_id_type=MESH,
        )

    def gram_copy(i):
        return pltpu.make_async_remote_copy(
            src_ref=gram.at[0], dst_ref=gram_in.at[i],
            send_sem=gram_send.at[i], recv_sem=gram_recv.at[i],
            device_id=(g, z, peers[i]), device_id_type=MESH,
        )

    def tile_copy(i):
        return pltpu.make_async_remote_copy(
            src_ref=tile, dst_ref=tile_in.at[i],
            send_sem=tile_send.at[i], recv_sem=tile_recv.at[i],
            device_id=(g, z, peers[i]), device_id_type=MESH,
        )

    def project(source, piece):
        part = contract_last(factors[source, 0, piece], rows[0, piece])
        part += contract_last(factors[source, 1, piece], rows[1, piece])
        side = (piece + pieces - n_left) // pieces
        proj[side, source] += part

    length = rows.shape[2] // 2
    total = 3 * pieces

    def step(k, carry):
        @pl.when(k < pieces)
        def _():
            for half in range(2):
                pltpu.make_async_copy(
                    left_ref.at[:, 0:width], factors.at[z, half, k], own_sem.at[half, k]
                ).wait()

        @pl.when(k < total)
        def _():
            @pl.when(is_inner)
            def _():
                @pl.when(k >= AHEAD)
                def _():
                    outward_copy(k - AHEAD).wait_send()
                outward_copy(k).start()

            @pl.when((k >= AHEAD) & (k < 2 * pieces + AHEAD))
            def _():
                inward_copy(k - AHEAD).wait_send()

            @pl.when(k < 2 * pieces)
            def _():
                inward_copy(k).start()

        @pl.when((k >= AHEAD) & (k < total + AHEAD))
        def _():
            j = k - AHEAD

            @pl.when(j < 2 * pieces + (1 - inner) * pieces)
            def _():
                arrival(j).wait_recv()
                swap_copy(j).start()

            @pl.when(j < 2 * pieces * inner)
            def _():
                minor_arrival(j).wait_recv()

        @pl.when(k < pieces)
        def _():
            for half in range(2):
                pltpu.make_async_copy(
                    grad_ref.at[:, 0:width], rows.at[half, k], row_sem.at[half, k]
                ).wait()
            project(z, k)
            side = (k + pieces - n_left) // pieces
            for seq in range(2):
                span = slice(seq * length, (seq + 1) * length)
                first, second = rows[0, k, span, :], rows[1, k, span, :]
                gram[side, span, :] += contract_last(first, first) + contract_last(second, second)

        @pl.when(k == n_left - 1)
        def _():
            for i in range(3):
                proj_copy(i, z).start()
                gram_copy(i).start()

        @pl.when(k >= AHEAD + SWAP)
        def _():
            j = k - AHEAD - SWAP

            @pl.when(j < 2 * pieces + (1 - inner) * pieces)
            def _():
                swap_copy(j).wait_send()
                swap_arrival(j).wait_recv()
            project(main_source(j), j % pieces)

            @pl.when(j % pieces == n_left - 1)
            def _():
                for i in range(3):
                    proj_copy(i, main_source(j)).start()
        return carry

    columns = proj.shape[2]
    share = columns // RANK
    token = lax.broadcasted_iota(jnp.int32, (1, length), 1)
    masks = [(token < counts_ref[seq]).astype(jnp.float32) for seq in range(2)]
    mask_row = jnp.concatenate(masks, axis=1)
    lane = lax.broadcasted_iota(jnp.int32, (8, 128), 1)
    sublane = lax.broadcasted_iota(jnp.int32, (8, 128), 0)

    def norm_terms():
        row_token = lax.broadcasted_iota(jnp.int32, (length, 1), 0)
        for i in range(3):
            gram_copy(i).wait_recv()
        kept = jnp.zeros((8, 128), jnp.float32)
        for seq in range(2):
            span = slice(seq * length, (seq + 1) * length)
            whole = gram[0, span, :] + gram_in[0, span, :] + gram_in[1, span, :] + gram_in[2, span, :]
            valid = (row_token < counts_ref[seq]).astype(jnp.float32)
            terms = whole * gram[1, span, :] * masks[seq] * valid
            down = jnp.sum(terms, axis=0, keepdims=True)
            kept += jnp.where(lane == 2 + seq, jnp.sum(down, axis=1, keepdims=True), 0.0)
        tile[...] = kept

    def take_projections(source):
        for i in range(3):
            proj_copy(i, source).wait_recv()
        whole = proj_in[0, source] + proj_in[1, source] + proj_in[2, source]
        full[source] = (proj[0, source] + whole) * mask_row

    def score_terms(source):
        terms = full[source] * proj[1, source]
        row = lax.broadcasted_iota(jnp.int32, (8, 2 * length), 0)
        for q in range(share):
            down = jnp.sum(terms[q * RANK:(q + 1) * RANK, :], axis=0, keepdims=True)
            found[...] += jnp.where(row == source * share + q, down, 0.0)

    found[...] = jnp.zeros_like(found)
    lax.fori_loop(0, total + AHEAD + SWAP - 2, step, 0)
    norm_terms()
    take_projections(z)
    score_terms(z)
    for phase in range(3):
        take_projections(main_source(phase * pieces))
    for phase in range(2):
        score_terms(main_source(phase * pieces))
    lax.fori_loop(total + AHEAD + SWAP - 2, total + AHEAD + SWAP, step, 0)
    score_terms(main_source(2 * pieces))
    mine = tile[...]
    for seq in range(2):
        span = slice(seq * length, (seq + 1) * length)
        value = jnp.sum(found[:, span], axis=1, keepdims=True)
        mine += jnp.where(lane == seq, value, 0.0)
    tile[...] = mine
    for i in range(3):
        tile_copy(i).start()
    for i in range(3):
        tile_copy(i).wait_recv()
    whole = tile[...] + tile_in[0] + tile_in[1] + tile_in[2]
    rms = jnp.sqrt(whole[0:1, 2:4] / (D * FF) + epsilon)
    for seq in range(2):
        score = jnp.sum(jnp.where(lane == sublane, whole[:, seq:seq + 1], 0.0), axis=0, keepdims=True)
        out_ref[seq:seq + 1, :] = score / rms[:, seq:seq + 1]
    out_ref[2:3, 0:2] = rms

    for k in range(AHEAD):
        @pl.when(is_inner)
        def _():
            outward_copy(total - 1 - k).wait_send()
    for i in range(3):
        tile_copy(i).wait_send()
        gram_copy(i).wait_send()
        for source in range(4):
            proj_copy(i, source).wait_send()


def take_out(result_ref, scores_ref, rms_ref):
    scores_ref[...] = result_ref[0:scores_ref.shape[0], 0:scores_ref.shape[1]]
    rms_ref[...] = result_ref[2:3, 0:rms_ref.shape[1]]


def piece_width(model_width, hidden_width):
    for width in (512, 256, 128):
        if model_width % (2 * width) == 0 and hidden_width % (2 * width) == 0:
            return width
    return 0


def line_shards(width, activations, output_gradients, counts, left_factors, right_factors):
    seq_dev, length, ff_local = activations.shape
    model_local = output_gradients.shape[2]
    row_count = seq_dev * length
    columns = left_factors.shape[0]
    n_left, n_right = model_local // (2 * width), ff_local // (2 * width)
    pieces = n_left + n_right
    dma = pltpu.SemaphoreType.DMA
    anywhere = pl.BlockSpec(memory_space=pl.ANY)
    vmem = pl.BlockSpec(memory_space=pltpu.VMEM)
    result = pl.pallas_call(
        functools.partial(line_kernel, n_left, n_right, width),
        out_shape=jax.ShapeDtypeStruct((8, 128), jnp.float32),
        in_specs=[pl.BlockSpec(memory_space=pltpu.SMEM)] + [anywhere] * 4,
        out_specs=vmem,
        scratch_shapes=[
            pltpu.VMEM((4, 2, pieces, columns, width), jnp.bfloat16),
            pltpu.VMEM((2, pieces, row_count, width), jnp.bfloat16),
            pltpu.VMEM((2, 4, columns, row_count), jnp.float32),
            pltpu.VMEM((2, row_count, length), jnp.float32),
            pltpu.VMEM((3, 4, columns, row_count), jnp.float32),
            pltpu.VMEM((3, row_count, length), jnp.float32),
            pltpu.VMEM((4, columns, row_count), jnp.float32),
            pltpu.VMEM((8, row_count), jnp.float32),
            pltpu.VMEM((8, 128), jnp.float32),
            pltpu.VMEM((3, 8, 128), jnp.float32),
            dma((2, pieces)),
            dma((2, pieces)),
            dma((3 * pieces,)),
            dma((2 * pieces,)),
            dma((2, 3 * pieces)),
            dma((3 * pieces,)),
            dma((3 * pieces,)),
            dma((3, 4)),
            dma((3, 4)),
            dma((3,)),
            dma((3,)),
            dma((3,)),
            dma((3,)),
        ],
        compiler_params=pltpu.CompilerParams(
            collective_id=0, has_side_effects=True, vmem_limit_bytes=60 * 2 ** 20
        ),
        cost_estimate=pl.CostEstimate(
            flops=2 * row_count * (4 * columns + length) * (model_local + ff_local),
            bytes_accessed=2 * (row_count + columns) * (model_local + ff_local),
            transcendentals=0,
        ),
    )(
        counts,
        activations.reshape(row_count, ff_local),
        output_gradients.reshape(row_count, model_local),
        left_factors,
        right_factors,
    )
    scores, rms = pl.pallas_call(
        take_out,
        out_shape=(
            jax.ShapeDtypeStruct((seq_dev, 4 * columns // RANK), jnp.float32),
            jax.ShapeDtypeStruct((1, seq_dev), jnp.float32),
        ),
    )(result)
    return scores, rms.reshape(seq_dev)


def shards(sizes, activations, output_gradients, counts, left_factors, right_factors):
    columns, model_local = left_factors.shape
    width = piece_width(model_local, right_factors.shape[1])
    fits = (
        sizes == (2, 4, 4)
        and width > 0
        and columns == 2 * RANK
        and right_factors.shape[1] // (2 * width) > AHEAD
        and activations.shape[:2] == (2, 128)
    )
    run = functools.partial(line_shards, width) if fits else plain_shards
    return run(activations, output_gradients, counts, left_factors, right_factors)


def solution(mesh):
    placed = (
        P(("groups", "dp"), None, "mp"),
        P(("groups", "dp"), None, "mp"),
        P(("groups", "dp")),
        P("dp", "mp"),
        P("dp", "mp"),
    )
    sizes = tuple(mesh.shape[name] for name in ("groups", "dp", "mp"))
    return jax.shard_map(
        functools.partial(shards, sizes),
        mesh=mesh,
        in_specs=placed,
        out_specs=(P(("groups", "dp"), None), P(("groups", "dp"))),
        check_vma=False,
    )
```

```python
import functools

import jax
import jax.numpy as jnp
from jax import lax
from jax.experimental import pallas as pl
from jax.experimental.pallas import tpu as pltpu
from jax.sharding import PartitionSpec as P

D = 8192
FF = 28672
RANK = 32
AHEAD = 5
SWAP = 3

epsilon = 1e-06
MESH = pl.DeviceIdType.MESH


def contract_last(left_side, right_side):
    return lax.dot_general(
        left_side, right_side, (((1,), (1,)), ((), ())), preferred_element_type=jnp.float32
    )


def plain_shards(activations, output_gradients, counts, left_factors, right_factors):
    seq_dev, length, ff_local = activations.shape
    local_model_width = output_gradients.shape[2]
    row_count = seq_dev * length
    act_rows = activations.reshape(row_count, ff_local)
    grad_rows = output_gradients.reshape(row_count, local_model_width)
    qcols_all = left_factors.shape[0] * lax.axis_size("dp")
    positions = lax.broadcasted_iota(jnp.int32, (seq_dev, length), 1)
    token_mask = (positions < counts[:, None]).astype(jnp.float32)
    pair_mask = token_mask[:, :, None] * token_mask[:, None, :]
    token_mask = token_mask.reshape(row_count)
    left_all, right_all = (
        lax.all_gather(left_factors, "dp", axis=0, tiled=True),
        lax.all_gather(right_factors, "dp", axis=0, tiled=True),
    )
    grad_proj = contract_last(grad_rows, left_all)
    act_proj = contract_last(act_rows, right_all)
    gradient_covariance = jnp.einsum(
        "anr,ayr->any", output_gradients, output_gradients, preferred_element_type=jnp.float32
    )
    act_gram = jnp.einsum(
        "slf,smf->slm", activations, activations, preferred_element_type=jnp.float32
    )
    grad_proj, gradient_covariance = lax.psum((grad_proj, gradient_covariance), "mp")
    token_terms = grad_proj * act_proj * token_mask[:, None]
    score_part = token_terms.reshape(seq_dev, length, qcols_all // RANK, RANK).sum(axis=(1, 3))
    norm_portion = jnp.sum(gradient_covariance * act_gram * pair_mask, axis=(1, 2))
    raw_score, norm_sq = lax.psum((score_part, norm_portion), "mp")
    grad_rms = jnp.sqrt(norm_sq / (D * FF) + epsilon)
    return (raw_score / grad_rms[:, None], grad_rms)


def line_kernel(
    n_left, n_right, width,
    counts_ref, act_ref, grad_ref, left_ref, right_ref,
    out_ref,
    factors, rows, proj, gram, proj_in, gram_in, full, found, tile, tile_in,
    own_sem, row_sem, out_send, in_send, line_recv, swap_send, swap_recv,
    proj_send, proj_recv, gram_send, gram_recv, tile_send, tile_recv,
):
    pieces = n_left + n_right
    g, z, m = lax.axis_index("groups"), lax.axis_index("dp"), lax.axis_index("mp")
    other = 1 - g
    step_in = 1 - 2 * (z // 2)
    inner = ((z + 1) // 2) % 2
    is_inner = inner == 1
    inward, outward = z + step_in, z - step_in
    peers = [lax.rem(m + i, 4) for i in (1, 2, 3)]

    def offset(half, piece):
        if piece < n_left:
            return (half * n_left + piece) * width
        return (half * n_right + piece - n_left) * width

    def factor_copy(half, piece):
        source, at = left_ref if piece < n_left else right_ref, offset(half, piece)
        return pltpu.make_async_copy(
            source.at[:, at:at + width], factors.at[z, half, piece], own_sem.at[half, piece]
        )

    def row_copy(half, piece):
        source, at = grad_ref if piece < n_left else act_ref, offset(half, piece)
        return pltpu.make_async_copy(
            source.at[:, at:at + width], rows.at[half, piece], row_sem.at[half, piece]
        )

    barrier = pltpu.get_barrier_semaphore()
    for i in range(3):
        pl.semaphore_signal(barrier, inc=1, device_id=(g, z, peers[i]), device_id_type=MESH)
    pl.semaphore_signal(barrier, inc=1, device_id=(other, z, m), device_id_type=MESH)
    pl.semaphore_signal(barrier, inc=1, device_id=(g, inward, m), device_id_type=MESH)

    @pl.when(is_inner)
    def _():
        pl.semaphore_signal(barrier, inc=1, device_id=(g, outward, m), device_id_type=MESH)

    everything = [(half, piece) for piece in range(pieces) for half in range(2)]
    for half, piece in everything:
        factor_copy(half, piece).start()

    proj[...] = jnp.zeros_like(proj)
    gram[...] = jnp.zeros_like(gram)
    pl.semaphore_wait(barrier, 5 + inner)

    def outward_copy(k):
        block = factors.at[(z + (k // pieces) * step_in) % 4, g, k % pieces]
        return pltpu.make_async_remote_copy(
            src_ref=block, dst_ref=block, send_sem=out_send.at[k], recv_sem=line_recv.at[0, k],
            device_id=(g, (outward + 4) % 4, m), device_id_type=MESH,
        )

    def inward_copy(k):
        late = k // pieces
        source = (z - late * inner * step_in + 4) % 4
        half = g + (1 - inner) * late * (1 - 2 * g)
        block = factors.at[source, half, k % pieces]
        return pltpu.make_async_remote_copy(
            src_ref=block, dst_ref=block, send_sem=in_send.at[k],
            recv_sem=line_recv.at[1 - inner, k],
            device_id=(g, inward, m), device_id_type=MESH,
        )

    def main_source(k):
        return (z + (k // pieces + 1) * step_in + 4) % 4

    def arrival(k):
        block = factors.at[main_source(k), g, k % pieces]
        return pltpu.make_async_remote_copy(
            src_ref=block, dst_ref=block, send_sem=out_send.at[k], recv_sem=line_recv.at[0, k],
            device_id=(g, inward, m), device_id_type=MESH,
        )

    def minor_arrival(k):
        late = k // pieces
        block = factors.at[(outward + 4) % 4, g + late * (1 - 2 * g), k % pieces]
        return pltpu.make_async_remote_copy(
            src_ref=block, dst_ref=block, send_sem=out_send.at[k], recv_sem=line_recv.at[1, k],
            device_id=(g, inward, m), device_id_type=MESH,
        )

    def swap_copy(k):
        block = factors.at[main_source(k), g, k % pieces]
        return pltpu.make_async_remote_copy(
            src_ref=block, dst_ref=block, send_sem=swap_send.at[k], recv_sem=swap_recv.at[k],
            device_id=(other, z, m), device_id_type=MESH,
        )

    def swap_arrival(k):
        block = factors.at[main_source(k), other, k % pieces]
        return pltpu.make_async_remote_copy(
            src_ref=block, dst_ref=block, send_sem=swap_send.at[k], recv_sem=swap_recv.at[k],
            device_id=(other, z, m), device_id_type=MESH,
        )

    def proj_copy(i, source):
        return pltpu.make_async_remote_copy(
            src_ref=proj.at[0, source], dst_ref=proj_in.at[i, source],
            send_sem=proj_send.at[i, source], recv_sem=proj_recv.at[i, source],
            device_id=(g, z, peers[i]), device_id_type=MESH,
        )

    def gram_copy(i):
        return pltpu.make_async_remote_copy(
            src_ref=gram.at[0], dst_ref=gram_in.at[i],
            send_sem=gram_send.at[i], recv_sem=gram_recv.at[i],
            device_id=(g, z, peers[i]), device_id_type=MESH,
        )

    def tile_copy(i):
        return pltpu.make_async_remote_copy(
            src_ref=tile, dst_ref=tile_in.at[i],
            send_sem=tile_send.at[i], recv_sem=tile_recv.at[i],
            device_id=(g, z, peers[i]), device_id_type=MESH,
        )

    def project(source, piece):
        part = contract_last(factors[source, 0, piece], rows[0, piece])
        part += contract_last(factors[source, 1, piece], rows[1, piece])
        side = (piece + pieces - n_left) // pieces
        proj[side, source] += part

    length = rows.shape[2] // 2
    total = 3 * pieces

    def send_step(k, carry):
        @pl.when(k < pieces)
        def _():
            for half in range(2):
                pltpu.make_async_copy(
                    left_ref.at[:, 0:width], factors.at[z, half, k], own_sem.at[half, k]
                ).wait()

        @pl.when(k < total)
        def _():
            @pl.when(is_inner)
            def _():
                @pl.when(k >= AHEAD)
                def _():
                    outward_copy(k - AHEAD).wait_send()
                outward_copy(k).start()

            @pl.when((k >= AHEAD) & (k < 2 * pieces + AHEAD))
            def _():
                inward_copy(k - AHEAD).wait_send()

            @pl.when(k < 2 * pieces)
            def _():
                inward_copy(k).start()

        return carry

    def step(k, carry):
        send_step(k + AHEAD, 0)

        @pl.when(k < total)
        def _():
            j = k

            @pl.when(j < 2 * pieces + (1 - inner) * pieces)
            def _():
                arrival(j).wait_recv()
                swap_copy(j).start()

            @pl.when(j < 2 * pieces * inner)
            def _():
                minor_arrival(j).wait_recv()

        @pl.when(k < pieces)
        def _():
            for half in range(2):
                pltpu.make_async_copy(
                    grad_ref.at[:, 0:width], rows.at[half, k], row_sem.at[half, k]
                ).wait()
            project(z, k)
            side = (k + pieces - n_left) // pieces
            for seq in range(2):
                span = slice(seq * length, (seq + 1) * length)
                first, second = rows[0, k, span, :], rows[1, k, span, :]
                gram[side, span, :] += contract_last(first, first) + contract_last(second, second)

        @pl.when(k == n_left - 1)
        def _():
            for i in range(3):
                proj_copy(i, z).start()
                gram_copy(i).start()

        @pl.when(k >= SWAP)
        def _():
            j = k - SWAP

            @pl.when(j < 2 * pieces + (1 - inner) * pieces)
            def _():
                swap_copy(j).wait_send()
                swap_arrival(j).wait_recv()
            project(main_source(j), j % pieces)

            @pl.when(j % pieces == n_left - 1)
            def _():
                for i in range(3):
                    proj_copy(i, main_source(j)).start()
        return carry

    columns = proj.shape[2]
    share = columns // RANK
    token = lax.broadcasted_iota(jnp.int32, (1, length), 1)
    masks = [(token < counts_ref[seq]).astype(jnp.float32) for seq in range(2)]
    mask_row = jnp.concatenate(masks, axis=1)
    lane = lax.broadcasted_iota(jnp.int32, (8, 128), 1)
    sublane = lax.broadcasted_iota(jnp.int32, (8, 128), 0)

    def norm_terms():
        row_token = lax.broadcasted_iota(jnp.int32, (length, 1), 0)
        for i in range(3):
            gram_copy(i).wait_recv()
        kept = jnp.zeros((8, 128), jnp.float32)
        for seq in range(2):
            span = slice(seq * length, (seq + 1) * length)
            whole = gram[0, span, :] + gram_in[0, span, :] + gram_in[1, span, :] + gram_in[2, span, :]
            valid = (row_token < counts_ref[seq]).astype(jnp.float32)
            terms = whole * gram[1, span, :] * masks[seq] * valid
            down = jnp.sum(terms, axis=0, keepdims=True)
            kept += jnp.where(lane == 2 + seq, jnp.sum(down, axis=1, keepdims=True), 0.0)
        tile[...] = kept

    def take_projections(source):
        for i in range(3):
            proj_copy(i, source).wait_recv()
        whole = proj_in[0, source] + proj_in[1, source] + proj_in[2, source]
        full[source] = (proj[0, source] + whole) * mask_row

    def score_terms(source):
        terms = full[source] * proj[1, source]
        row = lax.broadcasted_iota(jnp.int32, (8, 2 * length), 0)
        for q in range(share):
            down = jnp.sum(terms[q * RANK:(q + 1) * RANK, :], axis=0, keepdims=True)
            found[...] += jnp.where(row == source * share + q, down, 0.0)

    found[...] = jnp.zeros_like(found)
    lax.fori_loop(0, AHEAD, send_step, 0)
    for half, piece in everything:
        row_copy(half, piece).start()
    lax.fori_loop(0, total + SWAP - 2, step, 0)
    norm_terms()
    take_projections(z)
    score_terms(z)
    for phase in range(3):
        take_projections(main_source(phase * pieces))
    for phase in range(2):
        score_terms(main_source(phase * pieces))
    lax.fori_loop(total + SWAP - 2, total + SWAP, step, 0)
    score_terms(main_source(2 * pieces))
    mine = tile[...]
    for seq in range(2):
        span = slice(seq * length, (seq + 1) * length)
        value = jnp.sum(found[:, span], axis=1, keepdims=True)
        mine += jnp.where(lane == seq, value, 0.0)
    tile[...] = mine
    for i in range(3):
        tile_copy(i).start()
    for i in range(3):
        tile_copy(i).wait_recv()
    whole = tile[...] + tile_in[0] + tile_in[1] + tile_in[2]
    rms = jnp.sqrt(whole[0:1, 2:4] / (D * FF) + epsilon)
    for seq in range(2):
        score = jnp.sum(jnp.where(lane == sublane, whole[:, seq:seq + 1], 0.0), axis=0, keepdims=True)
        out_ref[seq:seq + 1, :] = score / rms[:, seq:seq + 1]
    out_ref[2:3, 0:2] = rms

    for k in range(AHEAD):
        @pl.when(is_inner)
        def _():
            outward_copy(total - 1 - k).wait_send()
    for i in range(3):
        tile_copy(i).wait_send()
        gram_copy(i).wait_send()
        for source in range(4):
            proj_copy(i, source).wait_send()


def take_out(result_ref, scores_ref, rms_ref):
    scores_ref[...] = result_ref[0:scores_ref.shape[0], 0:scores_ref.shape[1]]
    rms_ref[...] = result_ref[2:3, 0:rms_ref.shape[1]]


def piece_width(model_width, hidden_width):
    for width in (512, 256, 128):
        if model_width % (2 * width) == 0 and hidden_width % (2 * width) == 0:
            return width
    return 0


def line_shards(width, activations, output_gradients, counts, left_factors, right_factors):
    seq_dev, length, ff_local = activations.shape
    model_local = output_gradients.shape[2]
    row_count = seq_dev * length
    columns = left_factors.shape[0]
    n_left, n_right = model_local // (2 * width), ff_local // (2 * width)
    pieces = n_left + n_right
    dma = pltpu.SemaphoreType.DMA
    anywhere = pl.BlockSpec(memory_space=pl.ANY)
    vmem = pl.BlockSpec(memory_space=pltpu.VMEM)
    result = pl.pallas_call(
        functools.partial(line_kernel, n_left, n_right, width),
        out_shape=jax.ShapeDtypeStruct((8, 128), jnp.float32),
        in_specs=[pl.BlockSpec(memory_space=pltpu.SMEM)] + [anywhere] * 4,
        out_specs=vmem,
        scratch_shapes=[
            pltpu.VMEM((4, 2, pieces, columns, width), jnp.bfloat16),
            pltpu.VMEM((2, pieces, row_count, width), jnp.bfloat16),
            pltpu.VMEM((2, 4, columns, row_count), jnp.float32),
            pltpu.VMEM((2, row_count, length), jnp.float32),
            pltpu.VMEM((3, 4, columns, row_count), jnp.float32),
            pltpu.VMEM((3, row_count, length), jnp.float32),
            pltpu.VMEM((4, columns, row_count), jnp.float32),
            pltpu.VMEM((8, row_count), jnp.float32),
            pltpu.VMEM((8, 128), jnp.float32),
            pltpu.VMEM((3, 8, 128), jnp.float32),
            dma((2, pieces)),
            dma((2, pieces)),
            dma((3 * pieces,)),
            dma((2 * pieces,)),
            dma((2, 3 * pieces)),
            dma((3 * pieces,)),
            dma((3 * pieces,)),
            dma((3, 4)),
            dma((3, 4)),
            dma((3,)),
            dma((3,)),
            dma((3,)),
            dma((3,)),
        ],
        compiler_params=pltpu.CompilerParams(
            collective_id=0, has_side_effects=True, vmem_limit_bytes=60 * 2 ** 20
        ),
        cost_estimate=pl.CostEstimate(
            flops=2 * row_count * (4 * columns + length) * (model_local + ff_local),
            bytes_accessed=2 * (row_count + columns) * (model_local + ff_local),
            transcendentals=0,
        ),
    )(
        counts,
        activations.reshape(row_count, ff_local),
        output_gradients.reshape(row_count, model_local),
        left_factors,
        right_factors,
    )
    scores, rms = pl.pallas_call(
        take_out,
        out_shape=(
            jax.ShapeDtypeStruct((seq_dev, 4 * columns // RANK), jnp.float32),
            jax.ShapeDtypeStruct((1, seq_dev), jnp.float32),
        ),
    )(result)
    return scores, rms.reshape(seq_dev)


def shards(sizes, activations, output_gradients, counts, left_factors, right_factors):
    columns, model_local = left_factors.shape
    width = piece_width(model_local, right_factors.shape[1])
    fits = (
        sizes == (2, 4, 4)
        and width > 0
        and columns == 2 * RANK
        and right_factors.shape[1] // (2 * width) > AHEAD
        and activations.shape[:2] == (2, 128)
    )
    run = functools.partial(line_shards, width) if fits else plain_shards
    return run(activations, output_gradients, counts, left_factors, right_factors)


def solution(mesh):
    placed = (
        P(("groups", "dp"), None, "mp"),
        P(("groups", "dp"), None, "mp"),
        P(("groups", "dp")),
        P("dp", "mp"),
        P("dp", "mp"),
    )
    sizes = tuple(mesh.shape[name] for name in ("groups", "dp", "mp"))
    return jax.shard_map(
        functools.partial(shards, sizes),
        mesh=mesh,
        in_specs=placed,
        out_specs=(P(("groups", "dp"), None), P(("groups", "dp"))),
        check_vma=False,
    )
```
